256 devices in a mesh: dp: 32 (over y_hi, z, core), fsdp: 8 (over y_lo, x).
Axes of the slice: x: 4, y: 4 (y_hi: 2, y_lo: 2; y = y_hi * 2 + y_lo), z: 8, core: 2. Of those that a mesh axis runs over, the one named last changes fastest.
Arguments:
- hidden_act: bfloat16 [65536, 5120], P(('dp', 'fsdp')), may hold values from -6 to 6
- resid: bfloat16 [65536, 1280], P(('dp', 'fsdp')), may hold values from -6 to 6
- w_down: bfloat16 [5120, 1280], P('fsdp'), may hold values from -0.078125 to 0.078125
- norm_gain: float32 [1280], replicated, may hold values from 0.25 to 1.75
- w_proj: bfloat16 [1280, 1024], replicated, may hold values from -0.15625 to 0.15625
- optical: bfloat16 [1024, 1024], P(('dp', 'fsdp')), may hold values from -6 to 6
Outputs:
- d_hidden: bfloat16 [65536, 5120], P(('dp', 'fsdp'))
- d_resid: bfloat16 [65536, 1280], P(('dp', 'fsdp'))
- d_weight: float32 [5120, 1280], P('fsdp', 'dp')
The draws below stay inside these ranges and needn't reach their ends.
All inputs are finite; a program needn't handle non-finite values.
Results may differ from the reference program's by a relative error of at most 0.04.
Values may be sent and summed in bfloat16 or wider, within the bound.
No kernel may reach another device: no remote copies, remote signals or barrier semaphores. Data moves between devices by JAX's collectives and lax.ppermute only.
A program may use at most 128 MiB of HBM per device.

```python
import jax
import jax.numpy as jnp
from jax import lax

D = 1280
FF = 5120
E = 1024
PATCHES = 64
TOK_DEV = 256
PAIRS = 1024
TOKENS = 65536
DEVICES = 256


def draw_hidden_act(key, part):
    key = jax.random.fold_in(key, 13)
    base_key = jax.random.fold_in(key, 0)
    values = jax.random.normal(base_key, (TOKENS, FF), jnp.float32)
    return jnp.clip(values, -6.0, 6.0).astype(jnp.bfloat16)


def draw_optical(key, part):
    key = jax.random.fold_in(key, 11)
    noise_key = jax.random.fold_in(key, 0)
    noise = jax.random.normal(noise_key, (PAIRS, E), jnp.float32)
    values = noise
    return jnp.clip(values, -6.0, 6.0).astype(jnp.bfloat16)


def level_of(own_key, dims, pieces, low, top_value):
    level, own = 1.0, jax.random.fold_in(own_key, 6)
    for axis_at, shards_of in pieces:
        draws = jnp.exp(jax.random.uniform(jax.random.fold_in(own, axis_at), (shards_of,), jnp.float32, low / len(pieces), top_value / len(pieces)))
        level = level * jnp.repeat(draws, dims[axis_at] // shards_of).reshape([-1 if axis == axis_at else 1 for axis in range(len(dims))])
    return level


def centred(key, dims, deviation, reach, cuts=(), kind=jnp.bfloat16):
    result = deviation * jax.random.normal(key, dims, jnp.float32)
    if cuts:
        result = result * level_of(key, dims, cuts, -0.22, 0.18)
    return jnp.clip(result, -reach, reach).astype(kind)


def setup_inputs(seed: int = 0) -> dict:
    keys = jax.random.split(jax.random.key(seed), 7)
    return {
        "hidden_act": draw_hidden_act(jax.random.fold_in(keys[6], 71), 0),
        "resid": centred(keys[1], (TOKENS, D), 1.0, 6.0, ((0, 256),)),
        "w_down": centred(keys[2], (FF, D), FF ** -0.5, 0.078125, ((0, 8),)),
        "norm_gain": jnp.clip(1.0 + 0.15 * jax.random.normal(keys[3], (D,), jnp.float32), 0.25, 1.75),
        "w_proj": centred(keys[4], (D, E), D ** -0.5, 0.15625),
        "optical": draw_optical(jax.random.fold_in(keys[6], 71), 0),
    }


epsilon = 1e-06
logit_scale = 100.0

def reference(hidden_act, resid, w_down, norm_gain, w_proj, optical):
    branch = jnp.dot(hidden_act, w_down, preferred_element_type=jnp.float32)
    summed = resid.astype(jnp.float32) + branch
    center = lax.optimization_barrier(jnp.mean(summed, axis=1, keepdims=True))
    spread = lax.optimization_barrier(jnp.mean((summed - center) ** 2, axis=1, keepdims=True))
    inv_std = lax.rsqrt(spread + epsilon)
    normed = (summed - center) * inv_std
    scaled = normed * norm_gain
    pooled = scaled.reshape(PAIRS, PATCHES, D).mean(axis=1).astype(jnp.bfloat16)
    embed = jnp.dot(pooled, w_proj, preferred_element_type=jnp.float32)
    inv_len = lax.rsqrt(lax.optimization_barrier(jnp.sum(embed * embed, axis=1, keepdims=True)) + epsilon)
    sar_unit = embed * inv_len
    sar_half = sar_unit.astype(jnp.bfloat16)
    opt_full = optical.astype(jnp.float32)
    opt_unit = (opt_full * lax.rsqrt(lax.optimization_barrier(jnp.sum(opt_full * opt_full, axis=1, keepdims=True)) + epsilon)).astype(jnp.bfloat16)
    scores = logit_scale * jnp.dot(sar_half, opt_unit.T, preferred_element_type=jnp.float32)
    powers = jnp.exp(scores)
    row_prob = powers / lax.optimization_barrier(jnp.sum(powers, axis=1, keepdims=True))
    col_prob = powers / lax.optimization_barrier(jnp.sum(powers, axis=0, keepdims=True))
    weights = (row_prob + col_prob - 2.0 * jnp.eye(PAIRS, dtype=jnp.float32)).astype(jnp.bfloat16)
    grad_unit = 0.5 * logit_scale * jnp.dot(weights, opt_unit, preferred_element_type=jnp.float32)
    grad_embed = inv_len * (grad_unit - sar_unit * lax.optimization_barrier(jnp.sum(sar_unit * grad_unit, axis=1, keepdims=True)))
    grad_pooled = jnp.dot(grad_embed.astype(jnp.bfloat16), w_proj.T, preferred_element_type=jnp.float32)
    grad_tokens = jnp.repeat(grad_pooled / PATCHES, PATCHES, axis=0)
    grad_normed = grad_tokens * norm_gain
    grad_sum = inv_std * (grad_normed - lax.optimization_barrier(jnp.mean(grad_normed, axis=1, keepdims=True)) - normed * lax.optimization_barrier(jnp.mean(grad_normed * normed, axis=1, keepdims=True)))
    d_resid = grad_sum.astype(jnp.bfloat16)
    d_hidden = jnp.dot(d_resid, w_down.T, preferred_element_type=jnp.float32).astype(jnp.bfloat16)
    acts = hidden_act.reshape(DEVICES, TOK_DEV, FF)
    grads = d_resid.reshape(DEVICES, TOK_DEV, D)

    def accumulate(carry, pair_rows):
        term = jnp.dot(pair_rows[0].T, pair_rows[1], preferred_element_type=jnp.float32)
        return (carry + term.astype(jnp.bfloat16).astype(jnp.float32), None)
    d_weight, _ = lax.scan(accumulate, jnp.zeros((FF, D), jnp.float32), (acts, grads))
    return (d_hidden, d_resid, d_weight)
```

```python
import jax
import jax.numpy as jnp
from jax import lax
from jax.sharding import Mesh, PartitionSpec as P

PATCHES = 64
epsilon = 1e-06
logit_scale = 100.0
bf16 = jnp.bfloat16
f32 = jnp.float32
contract = (((1,), (1,)), ((), ()))
ALL = ("yh", "z", "c", "yl", "x")


def swap_core(v):
    return lax.ppermute(v, "c", [(0, 1), (1, 0)])


def total_sum(v):
    for axes in ("c", "x", ("yh", "yl"), "z"):
        v = lax.psum(v, axes)
    return v


def body(hidden_act, resid, w_down, norm_gain, w_proj, optical):
    tok_rows, ff = hidden_act.shape
    images = tok_rows // PATCHES
    width = resid.shape[1]
    half = width // 2
    shard = w_down.shape[0]
    core = lax.axis_index("c")

    w_part = lax.dynamic_slice_in_dim(w_down, core * half, half, 1)
    w_own = lax.all_gather(w_part, ("yl", "x"), axis=0, tiled=True)
    w_peer = swap_core(w_own)

    opt_full = optical.astype(f32)
    opt_unit = (
        opt_full * lax.rsqrt(jnp.sum(opt_full * opt_full, axis=1, keepdims=True) + epsilon)
    ).astype(bf16)
    every_opt = lax.all_gather(opt_unit, ("yl", "x"), axis=0, tiled=True)
    every_opt = lax.all_gather(every_opt, ("yh", "z", "c"), axis=0, tiled=True)

    hidden_peer = swap_core(hidden_act)

    branch_own = jnp.dot(hidden_act, w_own, preferred_element_type=f32)
    branch_peer = jnp.dot(hidden_act, w_peer, preferred_element_type=f32)
    first = core == 0
    branch = jnp.concatenate(
        [jnp.where(first, branch_own, branch_peer), jnp.where(first, branch_peer, branch_own)], axis=1
    )
    summed = resid.astype(f32) + branch
    center = jnp.mean(summed, axis=1, keepdims=True)
    spread = jnp.mean((summed - center) ** 2, axis=1, keepdims=True)
    inv_std = lax.rsqrt(spread + epsilon)
    normed = (summed - center) * inv_std
    scaled = normed * norm_gain
    pooled = scaled.reshape(images, PATCHES, width).mean(axis=1).astype(bf16)
    embed = jnp.dot(pooled, w_proj, preferred_element_type=f32)
    inv_len = lax.rsqrt(jnp.sum(embed * embed, axis=1, keepdims=True) + epsilon)
    sar_unit = embed * inv_len
    sar_half = sar_unit.astype(bf16)
    scores = logit_scale * lax.dot_general(
        sar_half, every_opt, contract, preferred_element_type=f32
    )
    powers = jnp.exp(scores)
    row_prob = powers / jnp.sum(powers, axis=1, keepdims=True)
    totals = total_sum(jnp.sum(powers, axis=0))
    col_prob = powers / totals[None, :]
    first_pair = lax.axis_index(ALL) * images
    positive = (
        lax.broadcasted_iota(jnp.int32, scores.shape, 1)
        == first_pair + lax.broadcasted_iota(jnp.int32, scores.shape, 0)
    ).astype(f32)
    weights = (row_prob + col_prob - 2.0 * positive).astype(bf16)
    grad_unit = 0.5 * logit_scale * jnp.dot(weights, every_opt, preferred_element_type=f32)
    grad_embed = inv_len * (
        grad_unit - sar_unit * jnp.sum(sar_unit * grad_unit, axis=1, keepdims=True)
    )
    grad_pooled = lax.dot_general(
        grad_embed.astype(bf16), w_proj, contract, preferred_element_type=f32
    )
    grad_tokens = jnp.broadcast_to(
        (grad_pooled / PATCHES)[:, None, :], (images, PATCHES, width)
    ).reshape(tok_rows, width)
    grad_normed = grad_tokens * norm_gain
    grad_sum = inv_std * (
        grad_normed
        - jnp.mean(grad_normed, axis=1, keepdims=True)
        - normed * jnp.mean(grad_normed * normed, axis=1, keepdims=True)
    )
    d_resid = grad_sum.astype(bf16)

    dp_rest = lax.axis_size("yh") * lax.axis_size("z")
    cols = width // (2 * dp_rest)
    place = lax.broadcasted_iota(jnp.int32, (width, width), 1)
    rest = lax.rem(place, half)
    which = lax.rem(place // half + core, 2)
    source = ((rest // cols) * 2 + which) * cols + lax.rem(rest, cols)
    pick = (lax.broadcasted_iota(jnp.int32, (width, width), 0) == source).astype(bf16)
    split = jnp.dot(d_resid, pick, preferred_element_type=f32).astype(bf16)
    d_cat = jnp.concatenate([split[:, :half], swap_core(split[:, half:])], axis=0)
    h_cat = jnp.concatenate([hidden_act, hidden_peer], axis=0)
    d_cat_t = d_cat.T
    terms = jnp.stack(
        [
            jnp.dot(
                d_cat_t, h_cat[:, k * shard : (k + 1) * shard], preferred_element_type=f32
            ).astype(bf16)
            for k in range(ff // shard)
        ]
    )
    group_sum = lax.psum_scatter(terms, ("yl", "x"), scatter_dimension=0, tiled=True)
    d_weight = lax.psum_scatter(
        group_sum.reshape(dp_rest, cols, shard), ("yh", "z"), scatter_dimension=0, tiled=True
    )
    d_weight = d_weight.reshape(cols, shard).astype(f32).T

    d_own = lax.dynamic_slice_in_dim(d_resid, core * half, half, 1)
    d_peer = lax.dynamic_slice_in_dim(d_resid, (1 - core) * half, half, 1)
    d_hidden = (
        lax.dot_general(d_own, w_own, contract, preferred_element_type=f32)
        + lax.dot_general(d_peer, w_peer, contract, preferred_element_type=f32)
    ).astype(bf16)
    return (d_hidden, d_resid, d_weight)


def solution(mesh):
    parts = Mesh(mesh.devices.reshape(2, -1, 2, 2, 4), ALL)
    rows = P(ALL, None)
    in_specs = (rows, rows, P(("yl", "x"), None), P(), P(), rows)
    out_specs = (rows, rows, P(("yl", "x"), ("yh", "z", "c")))
    return jax.shard_map(body, mesh=parts, in_specs=in_specs, out_specs=out_specs, check_vma=False)
```

```python
import jax
import jax.numpy as jnp
from jax import lax
from jax.sharding import Mesh, PartitionSpec as P

PATCHES = 64
epsilon = 1e-06
logit_scale = 100.0
bf16 = jnp.bfloat16
f32 = jnp.float32
contract = (((1,), (1,)), ((), ()))
ALL = ("yh", "z", "c", "yl", "x")
Y = ("yh", "yl")
TILE = 128
MAIN = 3 * TILE


def swap(v, axes, flip, size):
    return lax.ppermute(v, axes, [(i, i ^ flip) for i in range(size)])


def cswap(v):
    return swap(v, "c", 1, 2)


def xswap(v, flip):
    return swap(v, "x", flip, 4)


def yswap(v, flip):
    return swap(v, Y, flip, 4)


def zswap(v, flip):
    return swap(v, "z", flip, 8)


def cat(*parts, axis=0):
    return jnp.concatenate(parts, axis=axis)


def stage(*values):
    return lax.optimization_barrier(values)


def mm(a, b):
    return jnp.dot(a, b, preferred_element_type=f32)


def gray(k):
    return k ^ (k >> 1)


def gather(w_half, opt_unit, hidden, x, yl, yh):
    main = lax.all_gather(w_half[:, :MAIN], ("yl", "x"), axis=0, tiled=True)
    rows, shard = w_half.shape[0] // 2, w_half.shape[0]
    tiles = lax.dynamic_slice_in_dim(w_half, yh * rows, rows, 0)[None]
    q1, q2, o = tiles[:, :, MAIN : MAIN + TILE], tiles[:, :, MAIN + TILE :], opt_unit
    s1, s2, r1, r2, r3 = stage(xswap(q1, 1), xswap(q2, 3), xswap(o, 1), xswap(o, 2), xswap(o, 3))
    q1, q2, o = stage(cat(q1, s1), cat(q2, s2), cat(o, r1, r3, r2))
    s1, s2, r1, r2, r3 = stage(xswap(q1, 3), xswap(q2, 1), yswap(o, 1), yswap(o, 2), yswap(o, 3))
    o = cat(o, r1, r3, r2)
    size = o.shape[0]
    each = size // 16
    place = lax.broadcasted_iota(jnp.int32, (1, size), 1)
    y = yh * 2 + yl
    target = (
        (y ^ gray(lax.div(place, 4 * each))) * 4 + (x ^ gray(lax.rem(lax.div(place, each), 4)))
    ) * each + lax.rem(place, each)
    turn_rows = (lax.broadcasted_iota(jnp.int32, (size, size), 0) == target).astype(bf16)
    o = mm(turn_rows, o).astype(bf16)
    q1, q2, o, hidden = stage(cat(q1, s1), cat(q2[:1], s2[:1], q2[1:], s2[1:]), o, hidden)
    a1, a2, z1, z2, hidden_peer = stage(
        yswap(q1, 1), yswap(q2, 3), zswap(o, 1), zswap(o, 2), cswap(hidden)
    )
    m1, m2, o = stage(jnp.stack([q1, a1], axis=1), jnp.stack([q2, a2], axis=1), o)
    b1, b2, z3, z4, z5 = stage(
        yswap(m1, 3), yswap(m2, 1), zswap(o, 3), zswap(o, 4), zswap(o, 5)
    )
    other = b1[:, ::-1]
    q1 = cat(jnp.where(yh == 0, m1, other), jnp.where(yh == 0, other, m1), axis=2)
    mine = jnp.stack([q2, b2[:, 0]], axis=1)
    other = jnp.stack([b2[:, 1], a2], axis=1)
    q2 = cat(jnp.where(yh == 0, mine, other), jnp.where(yh == 0, other, mine), axis=2)
    q = cat(q1, q2, axis=3).reshape(8 * shard, 2 * TILE)
    side = cat(
        *[
            lax.dynamic_slice_in_dim(q, (gray(x ^ fx) * 2 + (yl ^ fy)) * shard, shard, 0)
            for fy in range(2)
            for fx in range(4)
        ]
    )
    opt_own = cat(o, z1, z2, z3, z4, z5, zswap(o, 6), zswap(o, 7))
    return main, side, opt_own, hidden_peer


def by_flip(v, flip):
    return cat(*[v[j ^ flip : (j ^ flip) + 1] for j in range(v.shape[0])])


def total_sum(v):
    flat = v.reshape(16, -1)
    flat = flat + by_flip(cswap(flat), 8)
    flat = flat + xswap(flat, 1) + xswap(flat, 2) + xswap(flat, 3)
    flat = flat + yswap(flat, 1)
    flat = flat + yswap(flat, 3)
    flat = flat + by_flip(zswap(flat, 1), 1)
    parts = [by_flip(zswap(flat, k), k) for k in (2, 4, 6)]
    return flat + parts[0] + parts[1] + parts[2]


def turn(core, yh, width, cols):
    half = width // 2
    place = lax.broadcasted_iota(jnp.int32, (width, 1), 0)
    rest = lax.rem(place, half)
    which = lax.div(place, half) ^ core
    pair = lax.div(rest, 4 * cols)
    up = lax.rem(lax.div(rest, 2 * cols), 2) ^ yh
    z = 2 * pair + lax.rem(lax.div(rest, cols), 2)
    source = ((up * 8 + z) * 2 + which) * cols + lax.rem(rest, cols)
    return (lax.broadcasted_iota(jnp.int32, (width, width), 1) == source).astype(bf16)


def reduce_weight(dt, hx, hy, unit, given, beside):
    rows = dt.shape[0] // 8
    two = 2 * rows
    q, h = 2 * unit, 4 * unit
    ta = mm(dt[: 2 * two], hx).astype(bf16)
    tb = mm(dt[2 * two :], hy).astype(bf16)
    a, b, c, d = ta[:two], ta[two:], tb[:two], tb[two:]
    m1, m2 = a[:, h:], b[:, q : q + h]
    m3, m4 = cat(c[:rows, h:], c[rows:, :h], axis=1), d[rows:]
    go, *_ = stage(given, m1, m2, m3, m4)
    ra, rb, rc, rd, done = stage(xswap(m1, 1), xswap(m2, 3), yswap(m3, 1), yswap(m4, 3), beside(go))
    sa = xswap(a[:, q:h] + ra[:, :q], 3)
    sb = xswap(b[:, q + h :] + rb[:, q:], 1)
    sc = yswap(c[rows:, h:] + rc[:, h:], 3)
    sd = yswap(d[:rows, h:] + rd[:, :h], 1)
    def add(*values):
        return sum(v.astype(f32) for v in values)

    ka = add(a[:, :q], ra[:, q:], sa)
    kb = add(b[:, :q], rb[:, :q], sb)
    kc = add(c[:rows, :h], rc[:, :h], sc)
    kd = add(d[:rows, :h], rd[:, h:], sd)
    ua = yswap(cat(ka[:rows, unit:], ka[rows:, :unit], axis=1).astype(bf16), 1)
    ub = yswap(kb[rows:].astype(bf16), 3)
    uc = xswap(kc[:, q:].astype(bf16), 1)
    ud = xswap(kd[:, unit : 3 * unit].astype(bf16), 3)
    va = yswap((ka[rows:, unit:] + ua[:, unit:]).astype(bf16), 3)
    vb = yswap((kb[:rows, unit:] + ub[:, :unit]).astype(bf16), 1)
    vc = xswap((kc[:, unit:q] + uc[:, :unit]).astype(bf16), 3)
    vd = xswap((kd[:, 3 * unit :] + ud[:, unit:]).astype(bf16), 1)
    out = [
        add(ka[:rows, :unit], ua[:, :unit], va),
        add(kb[:rows, :unit], ub[:, unit:], vb),
        add(kc[:, :unit], uc[:, unit:], vc),
        add(kd[:, :unit], ud[:, :unit], vd),
    ]
    return cat(*[v.astype(bf16) for v in out]).reshape(8, rows // 2, unit), done


def body(hidden_act, resid, w_down, norm_gain, w_proj, optical):
    tok_rows = hidden_act.shape[0]
    images = tok_rows // PATCHES
    width = resid.shape[1]
    half = width // 2
    shard = w_down.shape[0]
    cols = width // 32
    core, x, z, yl, yh = (lax.axis_index(a) for a in ("c", "x", "z", "yl", "yh"))

    opt_full = optical.astype(f32)
    opt_unit = (
        opt_full * lax.rsqrt(jnp.sum(opt_full * opt_full, axis=1, keepdims=True) + epsilon)
    ).astype(bf16)
    w_half = lax.dynamic_slice_in_dim(w_down, core * half, half, 1)
    main, side, opt_own, hidden_peer = gather(w_half, opt_unit, hidden_act, x, yl, yh)
    opt_peer = cswap(opt_own)
    both = cat(hidden_act, hidden_peer)
    pick = turn(core, yh, width, cols)
    main, both, pick, opt_peer = stage(main, both, pick, opt_peer)
    own = [main, side]
    peer = [cswap(v) for v in own]
    branch_own = [mm(hidden_act, v) for v in own]
    branch_peer = [mm(hidden_act, v) for v in peer]
    first = core == 0
    branch = cat(
        *[jnp.where(first, a, b) for a, b in zip(branch_own, branch_peer)],
        *[jnp.where(first, b, a) for a, b in zip(branch_own, branch_peer)],
        axis=1,
    )
    summed = resid.astype(f32) + branch
    center = jnp.mean(summed, axis=1, keepdims=True)
    spread = jnp.mean((summed - center) ** 2, axis=1, keepdims=True)
    inv_std = lax.rsqrt(spread + epsilon)
    normed = (summed - center) * inv_std
    scaled = normed * norm_gain
    pooled = scaled.reshape(images, PATCHES, width).mean(axis=1).astype(bf16)
    embed = jnp.dot(pooled, w_proj, preferred_element_type=f32)
    inv_len = lax.rsqrt(jnp.sum(embed * embed, axis=1, keepdims=True) + epsilon)
    sar_unit = embed * inv_len
    sar_half = sar_unit.astype(bf16)
    scores = logit_scale * cat(
        *[
            lax.dot_general(sar_half, v, contract, preferred_element_type=f32)
            for v in (opt_own, opt_peer)
        ],
        axis=1,
    )
    pairs = scores.shape[1]
    powers = jnp.exp(scores)
    row_prob = powers / jnp.sum(powers, axis=1, keepdims=True)
    totals = total_sum(jnp.sum(powers, axis=0)).reshape(1, -1)

    def lanes(xr, yr):
        return lax.dynamic_slice_in_dim(both, ((yl ^ yr) * 4 + (x ^ xr)) * shard, shard, 1)

    pieces = {(xr, yr): lanes(xr, yr) for xr in range(4) for yr in range(2)}
    hx = cat(*[pieces[xr, yr] for xr in (0, 3, 2, 1) for yr in range(2)], axis=1)
    hy = cat(*[pieces[xr, yr] for yr in range(2) for xr in (0, 3, 2, 1)], axis=1)
    totals, hx, hy = stage(totals, hx, hy)
    col_prob = powers / totals
    first_pair = ((yh * 2 + yl) * 4 + x) * images
    positive = (
        lax.broadcasted_iota(jnp.int32, scores.shape, 1)
        == first_pair + lax.broadcasted_iota(jnp.int32, scores.shape, 0)
    ).astype(f32)
    weights = (row_prob + col_prob - 2.0 * positive).astype(bf16)
    grad_unit = 0.5 * logit_scale * (
        mm(weights[:, : pairs // 2], opt_own) + mm(weights[:, pairs // 2 :], opt_peer)
    )
    grad_embed = inv_len * (
        grad_unit - sar_unit * jnp.sum(sar_unit * grad_unit, axis=1, keepdims=True)
    )
    grad_pooled = lax.dot_general(
        grad_embed.astype(bf16), w_proj, contract, preferred_element_type=f32
    )
    grad_tokens = jnp.broadcast_to(
        (grad_pooled / PATCHES)[:, None, :], (images, PATCHES, width)
    ).reshape(tok_rows, width)
    grad_normed = grad_tokens * norm_gain
    grad_sum = inv_std * (
        grad_normed
        - jnp.mean(grad_normed, axis=1, keepdims=True)
        - normed * jnp.mean(grad_normed * normed, axis=1, keepdims=True)
    )
    d_resid = grad_sum.astype(bf16)

    split = lax.dot_general(pick, d_resid, contract, preferred_element_type=f32).astype(bf16)
    dt = cat(split[:half], cswap(split[half:]), axis=1)

    def hidden_grad(d):
        result = 0.0
        for at, ws in ((core * half, own), ((1 - core) * half, peer)):
            part = lax.dynamic_slice_in_dim(d, at, half, 1)
            for piece, w in zip((part[:, :MAIN], part[:, MAIN:]), ws):
                result = result + lax.dot_general(piece, w, contract, preferred_element_type=f32)
        return result.astype(bf16)

    part, d_hidden = reduce_weight(dt, hx, hy, shard, d_resid, hidden_grad)
    d_weight = lax.dynamic_index_in_dim(part, z, 0, False).astype(f32)
    for flip in range(1, 8):
        d_weight = d_weight + zswap(lax.dynamic_index_in_dim(part, z ^ flip, 0, False), flip)
    return (d_hidden, d_resid, d_weight.T)


def solution(mesh):
    parts = Mesh(mesh.devices.reshape(2, -1, 2, 2, 4), ALL)
    rows = P(ALL, None)
    in_specs = (rows, rows, P(("yl", "x"), None), P(), P(), rows)
    out_specs = (rows, rows, P(("yl", "x"), ("yh", "z", "c")))
    return jax.shard_map(body, mesh=parts, in_specs=in_specs, out_specs=out_specs, check_vma=False)
```

```python
import jax
import jax.numpy as jnp
from jax import lax
from jax.sharding import Mesh, PartitionSpec as P

PATCHES = 64
epsilon = 1e-06
logit_scale = 100.0
bf16 = jnp.bfloat16
f32 = jnp.float32
contract = (((1,), (1,)), ((), ()))
ALL = ("yh", "z", "c", "yl", "x")
Y = ("yh", "yl")


def swap(v, axes, flip, size):
    return lax.ppermute(v, axes, [(i, i ^ flip) for i in range(size)])


def cswap(v):
    return swap(v, "c", 1, 2)


def xswap(v, flip):
    return swap(v, "x", flip, 4)


def yswap(v, flip):
    return swap(v, Y, flip, 4)


def zswap(v, flip):
    return swap(v, "z", flip, 8)


def cat(*parts, axis=0):
    return jnp.concatenate(parts, axis=axis)


def stage(*values):
    return lax.optimization_barrier(values)


def mm(a, b):
    return jnp.dot(a, b, preferred_element_type=f32)


def gray(k):
    return k ^ (k >> 1)


def one_hot(target):
    rows = lax.broadcasted_iota(jnp.int32, (target.shape[1], target.shape[1]), 0)
    return (rows == target).astype(bf16)


def gather(w_half, opt_unit, hidden, x, z, yl, yh):
    near = lax.all_gather(w_half, "x", axis=0, tiled=True)
    o = opt_unit
    r1, r2, r3 = stage(xswap(o, 1), xswap(o, 2), xswap(o, 3))
    o, w_half = stage(cat(o, r1, r3, r2), w_half)
    rows = w_half.shape[0] // 2
    w1, w2, r1, r2, r3 = stage(
        yswap(w_half[:rows], 1), yswap(w_half[rows:], 3), yswap(o, 1), yswap(o, 2), yswap(o, 3)
    )
    far = cat(w1, w2)
    o = cat(o, r1, r3, r2)
    each = o.shape[0] // 16
    place = lax.broadcasted_iota(jnp.int32, (1, 16 * each), 1)
    block = lax.div(place, each)
    to = ((yh * 2 + yl) ^ gray(lax.div(block, 4))) * 4 + (x ^ gray(lax.rem(block, 4)))
    o = mm(one_hot(to * each + lax.rem(place, each)), o).astype(bf16)
    o, hidden, far = stage(o, hidden, far)
    z1, z2, z3, hidden_peer = stage(zswap(o, 1), zswap(o, 2), zswap(o, 3), cswap(hidden))
    both = cat(hidden, hidden_peer)
    near, both, far, o, z1, z2, z3 = stage(near, both, far, o, z1, z2, z3)
    far = lax.all_gather(far, "x", axis=0, tiled=True)
    z4, z5, z6, z7, near_peer = stage(
        zswap(o, 4), zswap(o, 5), zswap(o, 6), zswap(o, 7), cswap(near)
    )
    o = cat(o, z1, z2, z3, z4, z5, z6, z7)
    each = o.shape[0] // 8
    place = lax.broadcasted_iota(jnp.int32, (1, 8 * each), 1)
    o = mm(one_hot((z ^ lax.div(place, each)) * each + lax.rem(place, each)), o).astype(bf16)
    return near, near_peer, far, o, both


def total_sum(v):
    v = v.reshape(8, -1)
    theirs = cswap(v)
    v = v + cat(theirs[4:], theirs[:4])
    v = v + xswap(v, 1) + xswap(v, 2) + xswap(v, 3)
    v = v + yswap(v, 1)
    v = v + yswap(v, 3)
    v = v + zswap(v, 1)
    v = v + zswap(v, 2) + zswap(v, 4) + zswap(v, 6)
    return v.reshape(1, -1)


def turn(core, yh, width, cols):
    half = width // 2
    place = lax.broadcasted_iota(jnp.int32, (width, 1), 0)
    rest = lax.rem(place, half)
    which = lax.div(place, half) ^ core
    pair = lax.div(rest, 4 * cols)
    up = lax.rem(lax.div(rest, 2 * cols), 2) ^ yh
    z = 2 * pair + lax.rem(lax.div(rest, cols), 2)
    source = ((up * 8 + z) * 2 + which) * cols + lax.rem(rest, cols)
    return (lax.broadcasted_iota(jnp.int32, (width, width), 1) == source).astype(bf16)


def reduce_weight(dt, hx, hy, unit, given, beside):
    rows = dt.shape[0] // 8
    two = 2 * rows
    q, h = 2 * unit, 4 * unit
    one, pair, three, four = [dt[k * two : (k + 1) * two] for k in range(4)]
    m1 = mm(one, hx[:, h:]).astype(bf16)
    m2 = mm(pair, hx[:, q : q + h]).astype(bf16)
    m3 = cat(mm(three[:rows], hy[:, h:]), mm(three[rows:], hy[:, :h]), axis=1).astype(bf16)
    m4 = mm(four[rows:], hy).astype(bf16)
    go, one, pair, three, four, *_ = stage(given, one, pair, three, four, m1, m2, m3, m4)
    ra, rb, rc, rd, done, a, b0, b1, c0, c1, d = stage(
        xswap(m1, 1),
        xswap(m2, 3),
        yswap(m3, 1),
        yswap(m4, 3),
        beside(go),
        mm(one, hx[:, :h]),
        mm(pair, hx[:, :q]),
        mm(pair, hx[:, q + h :]),
        mm(three[:rows], hy[:, :h]),
        mm(three[rows:], hy[:, h:]),
        mm(four[:rows], hy),
    )
    sa = xswap((a[:, q:] + ra[:, :q]).astype(bf16), 3)
    sb = xswap((b1 + rb[:, q:]).astype(bf16), 1)
    sc = yswap((c1 + rc[:, h:]).astype(bf16), 3)
    sd = yswap((d[:, h:] + rd[:, :h]).astype(bf16), 1)
    ka = a[:, :q] + ra[:, q:] + sa
    kb = b0 + rb[:, :q] + sb
    kc = c0 + rc[:, :h] + sc
    kd = d[:, :h] + rd[:, h:] + sd
    ua = yswap(cat(ka[:rows, unit:], ka[rows:, :unit], axis=1).astype(bf16), 1)
    ub = yswap(kb[rows:].astype(bf16), 3)
    uc = xswap(kc[:, q:].astype(bf16), 1)
    ud = xswap(kd[:, unit : 3 * unit].astype(bf16), 3)
    va = yswap((ka[rows:, unit:] + ua[:, unit:]).astype(bf16), 3)
    vb = yswap((kb[:rows, unit:] + ub[:, :unit]).astype(bf16), 1)
    vc = xswap((kc[:, unit:q] + uc[:, :unit]).astype(bf16), 3)
    vd = xswap((kd[:, 3 * unit :] + ud[:, unit:]).astype(bf16), 1)
    out = [
        ka[:rows, :unit] + ua[:, :unit] + va,
        kb[:rows, :unit] + ub[:, unit:] + vb,
        kc[:, :unit] + uc[:, unit:] + vc,
        kd[:, :unit] + ud[:, :unit] + vd,
    ]
    return cat(*[v.astype(bf16) for v in out]).reshape(8, rows // 2, unit), done


def body(hidden_act, resid, w_down, norm_gain, w_proj, optical):
    tok_rows = hidden_act.shape[0]
    images = tok_rows // PATCHES
    width = resid.shape[1]
    half = width // 2
    shard = w_down.shape[0]
    cols = width // 32
    core, x, z, yl, yh = (lax.axis_index(a) for a in ("c", "x", "z", "yl", "yh"))

    opt_full = optical.astype(f32)
    opt_unit = (
        opt_full * lax.rsqrt(jnp.sum(opt_full * opt_full, axis=1, keepdims=True) + epsilon)
    ).astype(bf16)
    w_half = lax.dynamic_slice_in_dim(w_down, core * half, half, 1)
    near, near_peer, far, opt_own, both = gather(w_half, opt_unit, hidden_act, x, z, yl, yh)
    opt_peer = cswap(opt_own)

    def lanes(xr, yr):
        return lax.dynamic_slice_in_dim(both, ((yl ^ yr) * 4 + (x ^ xr)) * shard, shard, 1)

    pieces = {(xr, yr): lanes(xr, yr) for xr in range(4) for yr in range(2)}
    hx = cat(*[pieces[xr, yr] for xr in (0, 3, 2, 1) for yr in range(2)], axis=1)
    hy = cat(*[pieces[xr, yr] for yr in range(2) for xr in (0, 3, 2, 1)], axis=1)
    pick = turn(core, yh, width, cols)
    group = 4 * shard
    h_near = lax.dynamic_slice_in_dim(hidden_act, yl * group, group, 1)
    h_far = lax.dynamic_slice_in_dim(hidden_act, (1 - yl) * group, group, 1)
    branch_own, branch_peer = mm(h_near, near), mm(h_near, near_peer)
    far, hx, hy, pick, opt_own, branch_own, branch_peer, h_far = stage(
        far, hx, hy, pick, opt_own, branch_own, branch_peer, h_far
    )
    far_peer = cswap(far)
    branch_own = branch_own + mm(h_far, far)
    branch_peer = branch_peer + mm(h_far, far_peer)
    first = core == 0
    branch = cat(
        jnp.where(first, branch_own, branch_peer), jnp.where(first, branch_peer, branch_own), axis=1
    )
    summed = resid.astype(f32) + branch
    center = jnp.mean(summed, axis=1, keepdims=True)
    spread = jnp.mean((summed - center) ** 2, axis=1, keepdims=True)
    inv_std = lax.rsqrt(spread + epsilon)
    normed = (summed - center) * inv_std
    scaled = normed * norm_gain
    pooled = scaled.reshape(images, PATCHES, width).mean(axis=1).astype(bf16)
    embed = jnp.dot(pooled, w_proj, preferred_element_type=f32)
    inv_len = lax.rsqrt(jnp.sum(embed * embed, axis=1, keepdims=True) + epsilon)
    sar_unit = embed * inv_len
    sar_half = sar_unit.astype(bf16)
    scores = logit_scale * cat(
        *[
            lax.dot_general(sar_half, v, contract, preferred_element_type=f32)
            for v in (opt_own, opt_peer)
        ],
        axis=1,
    )
    pairs = scores.shape[1]
    powers = jnp.exp(scores)
    row_prob = powers / jnp.sum(powers, axis=1, keepdims=True)
    totals = total_sum(jnp.sum(powers, axis=0))
    col_prob = powers / totals
    first_pair = (((z * 2 + yh) * 2 + yl) * 4 + x) * images
    positive = (
        lax.broadcasted_iota(jnp.int32, scores.shape, 1)
        == first_pair + lax.broadcasted_iota(jnp.int32, scores.shape, 0)
    ).astype(f32)
    weights = (row_prob + col_prob - 2.0 * positive).astype(bf16)
    grad_unit = 0.5 * logit_scale * (
        mm(weights[:, : pairs // 2], opt_own) + mm(weights[:, pairs // 2 :], opt_peer)
    )
    grad_embed = inv_len * (
        grad_unit - sar_unit * jnp.sum(sar_unit * grad_unit, axis=1, keepdims=True)
    )
    grad_pooled = lax.dot_general(
        grad_embed.astype(bf16), w_proj, contract, preferred_element_type=f32
    )
    grad_tokens = jnp.broadcast_to(
        (grad_pooled / PATCHES)[:, None, :], (images, PATCHES, width)
    ).reshape(tok_rows, width)
    grad_normed = grad_tokens * norm_gain
    grad_sum = inv_std * (
        grad_normed
        - jnp.mean(grad_normed, axis=1, keepdims=True)
        - normed * jnp.mean(grad_normed * normed, axis=1, keepdims=True)
    )
    d_resid = grad_sum.astype(bf16)

    split = lax.dot_general(pick, d_resid, contract, preferred_element_type=f32).astype(bf16)
    dt = cat(split[:half], cswap(split[half:]), axis=1)

    def hidden_grad(d):
        d_own = lax.dynamic_slice_in_dim(d, core * half, half, 1)
        d_peer = lax.dynamic_slice_in_dim(d, (1 - core) * half, half, 1)
        a, b = [
            (
                lax.dot_general(d_own, v, contract, preferred_element_type=f32)
                + lax.dot_general(d_peer, w, contract, preferred_element_type=f32)
            ).astype(bf16)
            for v, w in ((near, near_peer), (far, far_peer))
        ]
        return cat(jnp.where(yl == 0, a, b), jnp.where(yl == 0, b, a), axis=1)

    part, d_hidden = reduce_weight(dt, hx, hy, shard, d_resid, hidden_grad)
    d_weight = lax.dynamic_index_in_dim(part, z, 0, False).astype(f32)
    for flip in range(1, 8):
        d_weight = d_weight + zswap(lax.dynamic_index_in_dim(part, z ^ flip, 0, False), flip)
    return (d_hidden, d_resid, d_weight.T)


def solution(mesh):
    parts = Mesh(mesh.devices.reshape(2, -1, 2, 2, 4), ALL)
    rows = P(ALL, None)
    in_specs = (rows, rows, P(("yl", "x"), None), P(), P(), rows)
    out_specs = (rows, rows, P(("yl", "x"), ("yh", "z", "c")))
    return jax.shard_map(body, mesh=parts, in_specs=in_specs, out_specs=out_specs, check_vma=False)
```

```python
import jax
import jax.numpy as jnp
from jax import lax
from jax.sharding import Mesh, PartitionSpec as P

PATCHES = 64
epsilon = 1e-06
logit_scale = 100.0
bf16 = jnp.bfloat16
f32 = jnp.float32
contract = (((1,), (1,)), ((), ()))
ALL = ("yh", "z", "c", "yl", "x")
Y = ("yh", "yl")
SPLIT = 384


def swap(v, axes, flip, size):
    return lax.ppermute(v, axes, [(i, i ^ flip) for i in range(size)])


def cswap(v):
    return swap(v, "c", 1, 2)


def xswap(v, flip):
    return swap(v, "x", flip, 4)


def yswap(v, flip):
    return swap(v, Y, flip, 4)


def zswap(v, flip):
    return swap(v, "z", flip, 8)


def cat(*parts, axis=0):
    return jnp.concatenate(parts, axis=axis)


def stage(*values):
    return lax.optimization_barrier(values)


def mm(a, b):
    return jnp.dot(a, b, preferred_element_type=f32)


def gray(k):
    return k ^ (k >> 1)


def one_hot(target):
    rows = lax.broadcasted_iota(jnp.int32, (target.shape[1], target.shape[1]), 0)
    return (rows == target).astype(bf16)


def gather(w_half, opt_unit, hidden, others, x, z, yl, yh):
    near = lax.all_gather(w_half, "x", axis=0, tiled=True)
    o = opt_unit
    r1, r2, r3 = stage(xswap(o, 1), xswap(o, 2), xswap(o, 3))
    o, late = stage(cat(o, r1, r3, r2), w_half[SPLIT:])
    rows = late.shape[0] // 2
    w1, w2, r1, r2, r3 = stage(
        yswap(late[:rows], 1), yswap(late[rows:], 3), yswap(o, 1), yswap(o, 2), yswap(o, 3)
    )
    late = cat(w1, w2)
    o = cat(o, r1, r3, r2)
    each = o.shape[0] // 16
    place = lax.broadcasted_iota(jnp.int32, (1, 16 * each), 1)
    block = lax.div(place, each)
    to = ((yh * 2 + yl) ^ gray(lax.div(block, 4))) * 4 + (x ^ gray(lax.rem(block, 4)))
    o = mm(one_hot(to * each + lax.rem(place, each)), o).astype(bf16)
    o, hidden, late = stage(o, hidden, late)
    z1, z2, z3, z4, hidden_peer = stage(
        zswap(o, 1), zswap(o, 2), zswap(o, 3), zswap(o, 4), cswap(hidden)
    )
    near, o, late, z1, z2, z3, z4, hidden_peer, *others = stage(
        near, o, late, z1, z2, z3, z4, hidden_peer, *others
    )
    far2 = lax.all_gather(late, "x", axis=0, tiled=True)
    shards = near.reshape(4, -1, near.shape[1])[:, :SPLIT]
    f1, f2, near_peer, z5, z6 = stage(
        yswap(shards[:2], 1), yswap(shards[2:], 3), cswap(near), zswap(o, 5), zswap(o, 6)
    )
    both = cat(hidden, hidden_peer)
    z7 = zswap(o, 7)
    far1 = cat(f1, f2).reshape(4 * SPLIT, -1)
    o = cat(o, z1, z2, z3, z4, z5, z6, z7)
    each = o.shape[0] // 8
    place = lax.broadcasted_iota(jnp.int32, (1, 8 * each), 1)
    o = mm(one_hot((z ^ lax.div(place, each)) * each + lax.rem(place, each)), o).astype(bf16)
    return [near, far1, far2], [near_peer, cswap(far1), cswap(far2)], o, both, others


def total_sum(v):
    v = v.reshape(8, -1)
    theirs = cswap(v)
    v = v + cat(theirs[4:], theirs[:4])
    v = v + xswap(v, 1) + xswap(v, 2) + xswap(v, 3)
    v = v + yswap(v, 1)
    v = v + yswap(v, 3)
    v = v + zswap(v, 1)
    v = v + zswap(v, 2) + zswap(v, 4) + zswap(v, 6)
    return v.reshape(1, -1)


def turn(core, yh, z, width, cols):
    half = width // 2
    place = lax.broadcasted_iota(jnp.int32, (width, 1), 0)
    rest = lax.rem(place, half)
    which = lax.div(place, half) ^ core
    pair = lax.div(rest, 4 * cols)
    up = lax.rem(lax.div(rest, 2 * cols), 2) ^ yh ^ (pair == 3).astype(jnp.int32)
    at = (2 * pair + lax.rem(lax.div(rest, cols), 2)) ^ z
    source = ((up * 8 + at) * 2 + which) * cols + lax.rem(rest, cols)
    return (lax.broadcasted_iota(jnp.int32, (width, width), 1) == source).astype(bf16)


def reduce_weight(dt, hx, hy, unit, beside):
    rows = dt.shape[0] // 8
    two = 2 * rows
    q, h = 2 * unit, 4 * unit
    one, pair, last = dt[:two], dt[two : 2 * two], dt[4 * two - rows :]
    m1 = mm(one, hx[:, h:]).astype(bf16)
    m2 = mm(pair, hx[:, q : q + h]).astype(bf16)
    t = mm(dt[2 * two : 4 * two - rows], hy).astype(bf16)
    m3, m4 = cat(t[:rows, h:], t[rows:two, :h], axis=1), t[two:]
    given, work = beside
    go, one, pair, last, *_ = stage(given, one, pair, last, m1, m2, m3, m4)
    ra, rb, rc, rd, a, b, d, *done = stage(
        xswap(m1, 1),
        xswap(m2, 3),
        yswap(m3, 1),
        yswap(m4, 3),
        mm(one, hx[:, q:h]),
        mm(pair, hx[:, q + h :]),
        mm(last, hy[:, h:]),
        *work(go),
    )
    m1 = (a + ra[:, :q]).astype(bf16)
    m2 = (b + rb[:, q:]).astype(bf16)
    m3 = t[rows:two, h:] + rc[:, h:]
    m4 = (d + rd[:, :h]).astype(bf16)
    one, pair, last, *_ = stage(one, pair, last, m1, m2, m3, m4)
    sa, sb, sc, sd, a, b, d = stage(
        xswap(m1, 3),
        xswap(m2, 1),
        yswap(m3, 3),
        yswap(m4, 1),
        mm(one, hx[:, :q]),
        mm(pair, hx[:, :q]),
        mm(last, hy[:, :h]),
    )
    ka = a + ra[:, q:] + sa
    kb = b + rb[:, :q] + sb
    kc = t[:rows, :h].astype(f32) + rc[:, :h] + sc
    kd = d + rd[:, h:] + sd
    ua = yswap(cat(ka[:rows, unit:], ka[rows:, :unit], axis=1).astype(bf16), 1)
    ub = yswap(kb[rows:].astype(bf16), 3)
    uc = xswap(kc[:, q:].astype(bf16), 1)
    ud = xswap(kd[:, unit : 3 * unit].astype(bf16), 3)
    va = yswap((ka[rows:, unit:] + ua[:, unit:]).astype(bf16), 3)
    vb = yswap((kb[:rows, unit:] + ub[:, :unit]).astype(bf16), 1)
    vc = xswap((kc[:, unit:q] + uc[:, :unit]).astype(bf16), 3)
    vd = xswap((kd[:, 3 * unit :] + ud[:, unit:]).astype(bf16), 1)
    out = [
        ka[:rows, :unit] + ua[:, :unit] + va,
        kb[:rows, :unit] + ub[:, unit:] + vb,
        kc[:, :unit] + uc[:, unit:] + vc,
        kd[:, :unit] + ud[:, :unit] + vd,
    ]
    first = stage(out[0], *done)
    return [first[0]] + out[1:], first[1:]


def body(hidden_act, resid, w_down, norm_gain, w_proj, optical):
    tok_rows = hidden_act.shape[0]
    images = tok_rows // PATCHES
    width = resid.shape[1]
    half = width // 2
    shard = w_down.shape[0]
    cols = width // 32
    core, x, z, yl, yh = (lax.axis_index(a) for a in ("c", "x", "z", "yl", "yh"))

    opt_full = optical.astype(f32)
    opt_unit = (
        opt_full * lax.rsqrt(jnp.sum(opt_full * opt_full, axis=1, keepdims=True) + epsilon)
    ).astype(bf16)
    w_half = lax.dynamic_slice_in_dim(w_down, core * half, half, 1)
    pick = turn(core, yh, z, width, cols)
    group = 4 * shard
    h_near, h_far = [
        lax.dynamic_slice_in_dim(hidden_act, at * group, group, 1) for at in (yl, 1 - yl)
    ]
    h_parts = [h_near] + [
        cat(*[h_far[:, k * shard + low : k * shard + high] for k in range(4)], axis=1)
        for low, high in ((0, SPLIT), (SPLIT, shard))
    ]
    own, peer, opt_own, both, (pick, *h_parts) = gather(
        w_half, opt_unit, hidden_act, (pick, *h_parts), x, z, yl, yh
    )
    opt_peer = cswap(opt_own)

    def lanes(xr, yr):
        return lax.dynamic_slice_in_dim(both, ((yl ^ yr) * 4 + (x ^ xr)) * shard, shard, 1)

    pieces = {(xr, yr): lanes(xr, yr) for xr in range(4) for yr in range(2)}
    hx = cat(*[pieces[xr, yr] for xr in (0, 3, 2, 1) for yr in range(2)], axis=1)
    hy = cat(*[pieces[xr, yr] for yr in range(2) for xr in (0, 3, 2, 1)], axis=1)
    branch_own, branch_peer = mm(h_parts[0], own[0]), mm(h_parts[0], peer[0])
    far2, hx, hy, opt_own, branch_own, branch_peer, h_last = stage(
        own[2], hx, hy, opt_own, branch_own, branch_peer, h_parts[2]
    )
    branch_own = branch_own + mm(h_parts[1], own[1]) + mm(h_last, far2)
    branch_peer = branch_peer + mm(h_parts[1], peer[1]) + mm(h_last, peer[2])
    first = core == 0
    branch = cat(
        jnp.where(first, branch_own, branch_peer), jnp.where(first, branch_peer, branch_own), axis=1
    )
    summed = resid.astype(f32) + branch
    center = jnp.mean(summed, axis=1, keepdims=True)
    spread = jnp.mean((summed - center) ** 2, axis=1, keepdims=True)
    inv_std = lax.rsqrt(spread + epsilon)
    normed = (summed - center) * inv_std
    scaled = normed * norm_gain
    pooled = scaled.reshape(images, PATCHES, width).mean(axis=1).astype(bf16)
    embed = jnp.dot(pooled, w_proj, preferred_element_type=f32)
    inv_len = lax.rsqrt(jnp.sum(embed * embed, axis=1, keepdims=True) + epsilon)
    sar_unit = embed * inv_len
    sar_half = sar_unit.astype(bf16)
    scores = logit_scale * cat(
        *[
            lax.dot_general(sar_half, v, contract, preferred_element_type=f32)
            for v in (opt_own, opt_peer)
        ],
        axis=1,
    )
    pairs = scores.shape[1]
    powers = jnp.exp(scores)
    row_prob = powers / jnp.sum(powers, axis=1, keepdims=True)
    column = jnp.sum(powers, axis=0)
    totals = total_sum(column)
    col_prob = powers / totals
    first_pair = (((z * 2 + yh) * 2 + yl) * 4 + x) * images
    positive = (
        lax.broadcasted_iota(jnp.int32, scores.shape, 1)
        == first_pair + lax.broadcasted_iota(jnp.int32, scores.shape, 0)
    ).astype(f32)
    weights = (row_prob + col_prob - 2.0 * positive).astype(bf16)
    grad_unit = 0.5 * logit_scale * (
        mm(weights[:, : pairs // 2], opt_own) + mm(weights[:, pairs // 2 :], opt_peer)
    )
    grad_embed = inv_len * (
        grad_unit - sar_unit * jnp.sum(sar_unit * grad_unit, axis=1, keepdims=True)
    )
    grad_pooled = lax.dot_general(
        grad_embed.astype(bf16), w_proj, contract, preferred_element_type=f32
    )
    grad_tokens = jnp.broadcast_to(
        (grad_pooled / PATCHES)[:, None, :], (images, PATCHES, width)
    ).reshape(tok_rows, width)
    grad_normed = grad_tokens * norm_gain
    grad_sum = inv_std * (
        grad_normed
        - jnp.mean(grad_normed, axis=1, keepdims=True)
        - normed * jnp.mean(grad_normed * normed, axis=1, keepdims=True)
    )
    d_resid = grad_sum.astype(bf16)

    split, theirs = [
        lax.dot_general(v, d_resid, contract, preferred_element_type=f32).astype(bf16)
        for v in (pick[:half], pick[half:])
    ]
    dt = cat(split, cswap(theirs), axis=1)

    def hidden_grad(d):
        d_own = lax.dynamic_slice_in_dim(d, core * half, half, 1)
        d_peer = lax.dynamic_slice_in_dim(d, (1 - core) * half, half, 1)
        return [
            (
                lax.dot_general(d_own, v, contract, preferred_element_type=f32)
                + lax.dot_general(d_peer, w, contract, preferred_element_type=f32)
            ).astype(bf16)
            for v, w in zip(own, peer)
        ]

    parts, d_parts = reduce_weight(
        dt, hx, hy, shard, (d_resid, hidden_grad)
    )
    d_weight = parts[0][:cols]
    for flip in range(1, 8):
        block = parts[flip // 2][flip % 2 * cols :][:cols].astype(bf16)
        d_weight = d_weight + zswap(block, flip)
    a, v, w = d_parts
    low, high = SPLIT, shard - SPLIT
    b = cat(
        *[
            p
            for k in range(4)
            for p in (v[:, k * low : (k + 1) * low], w[:, k * high : (k + 1) * high])
        ],
        axis=1,
    )
    d_hidden = cat(jnp.where(yl == 0, a, b), jnp.where(yl == 0, b, a), axis=1)
    return (d_hidden, d_resid, d_weight.T)


def solution(mesh):
    parts = Mesh(mesh.devices.reshape(2, -1, 2, 2, 4), ALL)
    rows = P(ALL, None)
    in_specs = (rows, rows, P(("yl", "x"), None), P(), P(), rows)
    out_specs = (rows, rows, P(("yl", "x"), ("yh", "z", "c")))
    return jax.shard_map(body, mesh=parts, in_specs=in_specs, out_specs=out_specs, check_vma=False)
```

```python
import jax
import jax.numpy as jnp
from jax import lax
from jax.sharding import Mesh, PartitionSpec as P

PATCHES = 64
epsilon = 1e-06
logit_scale = 100.0
bf16 = jnp.bfloat16
f32 = jnp.float32
contract = (((1,), (1,)), ((), ()))
ALL = ("yh", "z", "c", "yl", "x")
Y = ("yh", "yl")


def swap(v, axes, flip, size):
    return lax.ppermute(v, axes, [(i, i ^ flip) for i in range(size)])


def cswap(v):
    return swap(v, "c", 1, 2)


def xswap(v, flip):
    return swap(v, "x", flip, 4)


def yswap(v, flip):
    return swap(v, Y, flip, 4)


def zswap(v, flip):
    return swap(v, "z", flip, 8)


def cat(*parts, axis=0):
    return jnp.concatenate(parts, axis=axis)


def stage(*values):
    return lax.optimization_barrier(values)


def mm(a, b):
    return jnp.dot(a, b, preferred_element_type=f32)


def gray(k):
    return k ^ (k >> 1)


def one_hot(target):
    rows = lax.broadcasted_iota(jnp.int32, (target.shape[1], target.shape[1]), 0)
    return (rows == target).astype(bf16)


def gather(w_half, opt_unit, hidden, x, z, yl, yh):
    near = lax.all_gather(w_half, "x", axis=0, tiled=True)
    o = opt_unit
    r1, r2, r3 = stage(xswap(o, 1), xswap(o, 2), xswap(o, 3))
    o, w_half = stage(cat(o, r1, r3, r2), w_half)
    rows = w_half.shape[0] // 2
    w1, w2, r1, r2, r3 = stage(
        yswap(w_half[:rows], 1), yswap(w_half[rows:], 3), yswap(o, 1), yswap(o, 2), yswap(o, 3)
    )
    far = cat(w1, w2)
    o = cat(o, r1, r3, r2)
    each = o.shape[0] // 16
    place = lax.broadcasted_iota(jnp.int32, (1, 16 * each), 1)
    block = lax.div(place, each)
    to = ((yh * 2 + yl) ^ gray(lax.div(block, 4))) * 4 + (x ^ gray(lax.rem(block, 4)))
    o = mm(one_hot(to * each + lax.rem(place, each)), o).astype(bf16)
    o, hidden, far = stage(o, hidden, far)
    z1, z2, z3, hidden_peer = stage(zswap(o, 1), zswap(o, 2), zswap(o, 3), cswap(hidden))
    both = cat(hidden, hidden_peer)
    near, both, far, o, z1, z2, z3 = stage(near, both, far, o, z1, z2, z3)
    far = lax.all_gather(far, "x", axis=0, tiled=True)
    z4, z5, z6, z7, near_peer = stage(
        zswap(o, 4), zswap(o, 5), zswap(o, 6), zswap(o, 7), cswap(near)
    )
    o = cat(o, z1, z2, z3, z4, z5, z6, z7)
    each = o.shape[0] // 8
    place = lax.broadcasted_iota(jnp.int32, (1, 8 * each), 1)
    o = mm(one_hot((z ^ lax.div(place, each)) * each + lax.rem(place, each)), o).astype(bf16)
    return near, near_peer, far, o, both


def total_sum(v):
    v = v.reshape(8, -1)
    theirs = cswap(v)
    v = v + cat(theirs[4:], theirs[:4])
    v = v + xswap(v, 1) + xswap(v, 2) + xswap(v, 3)
    v = v + yswap(v, 1)
    v = v + yswap(v, 3)
    v = v + zswap(v, 1)
    v = v + zswap(v, 2) + zswap(v, 4) + zswap(v, 6)
    return v.reshape(1, -1)


def turn(core, yh, z, width, cols):
    half = width // 2
    place = lax.broadcasted_iota(jnp.int32, (width, 1), 0)
    rest = lax.rem(place, half)
    which = lax.div(place, half) ^ core
    pair = lax.div(rest, 4 * cols)
    up = lax.rem(lax.div(rest, 2 * cols), 2) ^ yh ^ (pair == 3).astype(jnp.int32)
    at = (2 * pair + lax.rem(lax.div(rest, cols), 2)) ^ z
    source = ((up * 8 + at) * 2 + which) * cols + lax.rem(rest, cols)
    return (lax.broadcasted_iota(jnp.int32, (width, width), 1) == source).astype(bf16)


def reduce_weight(dt, hx, hy, unit, beside):
    rows = dt.shape[0] // 8
    two = 2 * rows
    q, h = 2 * unit, 4 * unit
    one, pair, last = dt[:two], dt[two : 2 * two], dt[4 * two - rows :]
    m1 = mm(one, hx[:, h:]).astype(bf16)
    m2 = mm(pair, hx[:, q : q + h]).astype(bf16)
    t = mm(dt[2 * two : 4 * two - rows], hy).astype(bf16)
    m3, m4 = cat(t[:rows, h:], t[rows:two, :h], axis=1), t[two:]
    given, work = beside
    go, one, pair, last, *_ = stage(given, one, pair, last, m1, m2, m3, m4)
    ra, rb, rc, rd, a, b, d, *done = stage(
        xswap(m1, 1),
        xswap(m2, 3),
        yswap(m3, 1),
        yswap(m4, 3),
        mm(one, hx[:, q:h]),
        mm(pair, hx[:, q + h :]),
        mm(last, hy[:, h:]),
        *work(go),
    )
    m1 = (a + ra[:, :q]).astype(bf16)
    m2 = (b + rb[:, q:]).astype(bf16)
    m3 = t[rows:two, h:] + rc[:, h:]
    m4 = (d + rd[:, :h]).astype(bf16)
    one, pair, last, *_ = stage(one, pair, last, m1, m2, m3, m4)
    sa, sb, sc, sd, a, b, d = stage(
        xswap(m1, 3),
        xswap(m2, 1),
        yswap(m3, 3),
        yswap(m4, 1),
        mm(one, hx[:, :q]),
        mm(pair, hx[:, :q]),
        mm(last, hy[:, :h]),
    )
    ka = a + ra[:, q:] + sa
    kb = b + rb[:, :q] + sb
    kc = t[:rows, :h].astype(f32) + rc[:, :h] + sc
    kd = d + rd[:, h:] + sd
    ua = yswap(cat(ka[:rows, unit:], ka[rows:, :unit], axis=1).astype(bf16), 1)
    ub = yswap(kb[rows:].astype(bf16), 3)
    uc = xswap(kc[:, q:].astype(bf16), 1)
    ud = xswap(kd[:, unit : 3 * unit].astype(bf16), 3)
    va = yswap((ka[rows:, unit:] + ua[:, unit:]).astype(bf16), 3)
    vb = yswap((kb[:rows, unit:] + ub[:, :unit]).astype(bf16), 1)
    vc = xswap((kc[:, unit:q] + uc[:, :unit]).astype(bf16), 3)
    vd = xswap((kd[:, 3 * unit :] + ud[:, unit:]).astype(bf16), 1)
    out = [
        ka[:rows, :unit] + ua[:, :unit] + va,
        kb[:rows, :unit] + ub[:, unit:] + vb,
        kc[:, :unit] + uc[:, unit:] + vc,
        kd[:, :unit] + ud[:, :unit] + vd,
    ]
    first = stage(out[0], *done)
    return [first[0]] + out[1:], first[1:]


def body(hidden_act, resid, w_down, norm_gain, w_proj, optical):
    tok_rows = hidden_act.shape[0]
    images = tok_rows // PATCHES
    width = resid.shape[1]
    half = width // 2
    shard = w_down.shape[0]
    cols = width // 32
    core, x, z, yl, yh = (lax.axis_index(a) for a in ("c", "x", "z", "yl", "yh"))

    opt_full = optical.astype(f32)
    opt_unit = (
        opt_full * lax.rsqrt(jnp.sum(opt_full * opt_full, axis=1, keepdims=True) + epsilon)
    ).astype(bf16)
    w_half = lax.dynamic_slice_in_dim(w_down, core * half, half, 1)
    near, near_peer, far, opt_own, both = gather(w_half, opt_unit, hidden_act, x, z, yl, yh)
    opt_peer = cswap(opt_own)

    def lanes(xr, yr):
        return lax.dynamic_slice_in_dim(both, ((yl ^ yr) * 4 + (x ^ xr)) * shard, shard, 1)

    pieces = {(xr, yr): lanes(xr, yr) for xr in range(4) for yr in range(2)}
    hx = cat(*[pieces[xr, yr] for xr in (0, 3, 2, 1) for yr in range(2)], axis=1)
    hy = cat(*[pieces[xr, yr] for yr in range(2) for xr in (0, 3, 2, 1)], axis=1)
    pick = turn(core, yh, z, width, cols)
    group = 4 * shard
    h_near = lax.dynamic_slice_in_dim(hidden_act, yl * group, group, 1)
    h_far = lax.dynamic_slice_in_dim(hidden_act, (1 - yl) * group, group, 1)
    branch_own, branch_peer = mm(h_near, near), mm(h_near, near_peer)
    far, hx, hy, pick, opt_own, branch_own, branch_peer, h_far = stage(
        far, hx, hy, pick, opt_own, branch_own, branch_peer, h_far
    )
    far_peer = cswap(far)
    branch_own = branch_own + mm(h_far, far)
    branch_peer = branch_peer + mm(h_far, far_peer)
    first = core == 0
    branch = cat(
        jnp.where(first, branch_own, branch_peer), jnp.where(first, branch_peer, branch_own), axis=1
    )
    summed = resid.astype(f32) + branch
    center = jnp.mean(summed, axis=1, keepdims=True)
    spread = jnp.mean((summed - center) ** 2, axis=1, keepdims=True)
    inv_std = lax.rsqrt(spread + epsilon)
    normed = (summed - center) * inv_std
    scaled = normed * norm_gain
    pooled = scaled.reshape(images, PATCHES, width).mean(axis=1).astype(bf16)
    embed = jnp.dot(pooled, w_proj, preferred_element_type=f32)
    inv_len = lax.rsqrt(jnp.sum(embed * embed, axis=1, keepdims=True) + epsilon)
    sar_unit = embed * inv_len
    sar_half = sar_unit.astype(bf16)
    scores = logit_scale * cat(
        *[
            lax.dot_general(sar_half, v, contract, preferred_element_type=f32)
            for v in (opt_own, opt_peer)
        ],
        axis=1,
    )
    pairs = scores.shape[1]
    powers = jnp.exp(scores)
    row_prob = powers / jnp.sum(powers, axis=1, keepdims=True)
    column = jnp.sum(powers, axis=0)
    totals = total_sum(column)
    col_prob = powers / totals
    first_pair = (((z * 2 + yh) * 2 + yl) * 4 + x) * images
    positive = (
        lax.broadcasted_iota(jnp.int32, scores.shape, 1)
        == first_pair + lax.broadcasted_iota(jnp.int32, scores.shape, 0)
    ).astype(f32)
    weights = (row_prob + col_prob - 2.0 * positive).astype(bf16)
    grad_unit = 0.5 * logit_scale * (
        mm(weights[:, : pairs // 2], opt_own) + mm(weights[:, pairs // 2 :], opt_peer)
    )
    grad_embed = inv_len * (
        grad_unit - sar_unit * jnp.sum(sar_unit * grad_unit, axis=1, keepdims=True)
    )
    grad_pooled = lax.dot_general(
        grad_embed.astype(bf16), w_proj, contract, preferred_element_type=f32
    )
    grad_tokens = jnp.broadcast_to(
        (grad_pooled / PATCHES)[:, None, :], (images, PATCHES, width)
    ).reshape(tok_rows, width)
    grad_normed = grad_tokens * norm_gain
    grad_sum = inv_std * (
        grad_normed
        - jnp.mean(grad_normed, axis=1, keepdims=True)
        - normed * jnp.mean(grad_normed * normed, axis=1, keepdims=True)
    )
    d_resid = grad_sum.astype(bf16)

    split, theirs = [
        lax.dot_general(v, d_resid, contract, preferred_element_type=f32).astype(bf16)
        for v in (pick[:half], pick[half:])
    ]
    dt = cat(split, cswap(theirs), axis=1)

    def hidden_grad(d):
        d_own = lax.dynamic_slice_in_dim(d, core * half, half, 1)
        d_peer = lax.dynamic_slice_in_dim(d, (1 - core) * half, half, 1)
        return [
            (
                lax.dot_general(d_own, v, contract, preferred_element_type=f32)
                + lax.dot_general(d_peer, w, contract, preferred_element_type=f32)
            ).astype(bf16)
            for v, w in ((near, near_peer), (far, far_peer))
        ]

    parts, d_parts = reduce_weight(
        dt, hx, hy, shard, (d_resid, hidden_grad)
    )
    d_weight = parts[0][:cols]
    for flip in range(1, 8):
        block = parts[flip // 2][flip % 2 * cols :][:cols].astype(bf16)
        d_weight = d_weight + zswap(block, flip)
    a, b = d_parts
    d_hidden = cat(jnp.where(yl == 0, a, b), jnp.where(yl == 0, b, a), axis=1)
    return (d_hidden, d_resid, d_weight.T)


def solution(mesh):
    parts = Mesh(mesh.devices.reshape(2, -1, 2, 2, 4), ALL)
    rows = P(ALL, None)
    in_specs = (rows, rows, P(("yl", "x"), None), P(), P(), rows)
    out_specs = (rows, rows, P(("yl", "x"), ("yh", "z", "c")))
    return jax.shard_map(body, mesh=parts, in_specs=in_specs, out_specs=out_specs, check_vma=False)
```

```python
import jax
import jax.numpy as jnp
from jax import lax
from jax.sharding import Mesh, PartitionSpec as P

PATCHES = 64
epsilon = 1e-06
logit_scale = 100.0
bf16 = jnp.bfloat16
f32 = jnp.float32
contract = (((1,), (1,)), ((), ()))
ALL = ("yh", "z", "c", "yl", "x")
Y = ("yh", "yl")


def swap(v, axes, flip, size):
    return lax.ppermute(v, axes, [(i, i ^ flip) for i in range(size)])


def cswap(v):
    return swap(v, "c", 1, 2)


def xswap(v, flip):
    return swap(v, "x", flip, 4)


def yswap(v, flip):
    return swap(v, Y, flip, 4)


def zswap(v, flip):
    return swap(v, "z", flip, 8)


def cat(*parts, axis=0):
    return jnp.concatenate(parts, axis=axis)


def stage(*values):
    return lax.optimization_barrier(values)


def mm(a, b):
    return jnp.dot(a, b, preferred_element_type=f32)


def gray(k):
    return k ^ (k >> 1)


def one_hot(target):
    rows = lax.broadcasted_iota(jnp.int32, (target.shape[1], target.shape[1]), 0)
    return (rows == target).astype(bf16)


def gather(w_half, opt_unit, hidden, x, z, yl, yh):
    near = lax.all_gather(w_half, "x", axis=0, tiled=True)
    o = opt_unit
    r1, r2, r3 = stage(xswap(o, 1), xswap(o, 2), xswap(o, 3))
    o, w_half = stage(cat(o, r1, r3, r2), w_half)
    rows = w_half.shape[0] // 2
    w1, w2, r1, r2, r3 = stage(
        yswap(w_half[:rows], 1), yswap(w_half[rows:], 3), yswap(o, 1), yswap(o, 2), yswap(o, 3)
    )
    far = cat(w1, w2)
    o = cat(o, r1, r3, r2)
    each = o.shape[0] // 16
    place = lax.broadcasted_iota(jnp.int32, (1, 16 * each), 1)
    block = lax.div(place, each)
    to = ((yh * 2 + yl) ^ gray(lax.div(block, 4))) * 4 + (x ^ gray(lax.rem(block, 4)))
    o = mm(one_hot(to * each + lax.rem(place, each)), o).astype(bf16)
    o, hidden, far = stage(o, hidden, far)
    z1, z2, z3, hidden_peer = stage(zswap(o, 1), zswap(o, 2), zswap(o, 3), cswap(hidden))
    both = cat(hidden, hidden_peer)
    near, both, far, o, z1, z2, z3 = stage(near, both, far, o, z1, z2, z3)
    far = lax.all_gather(far, "x", axis=0, tiled=True)
    z4, z5, z6, z7, near_peer = stage(
        zswap(o, 4), zswap(o, 5), zswap(o, 6), zswap(o, 7), cswap(near)
    )
    o = cat(o, z1, z2, z3, z4, z5, z6, z7)
    each = o.shape[0] // 8
    place = lax.broadcasted_iota(jnp.int32, (1, 8 * each), 1)
    o = mm(one_hot((z ^ lax.div(place, each)) * each + lax.rem(place, each)), o).astype(bf16)
    return near, near_peer, far, o, both


def total_sum(v):
    v = v.reshape(8, -1)
    theirs = cswap(v)
    v = v + cat(theirs[4:], theirs[:4])
    v = v + xswap(v, 1) + xswap(v, 2) + xswap(v, 3)
    v = v + yswap(v, 1)
    v = v + yswap(v, 3)
    v = v + zswap(v, 1)
    v = v + zswap(v, 2) + zswap(v, 4) + zswap(v, 6)
    return v.reshape(1, -1)


def turn(core, yh, z, width, cols):
    half = width // 2
    place = lax.broadcasted_iota(jnp.int32, (width, 1), 0)
    rest = lax.rem(place, half)
    which = lax.div(place, half) ^ core
    pair = lax.div(rest, 4 * cols)
    up = lax.rem(lax.div(rest, 2 * cols), 2) ^ yh ^ (pair == 3).astype(jnp.int32)
    at = (2 * pair + lax.rem(lax.div(rest, cols), 2)) ^ z
    source = ((up * 8 + at) * 2 + which) * cols + lax.rem(rest, cols)
    return (lax.broadcasted_iota(jnp.int32, (width, width), 1) == source).astype(bf16)


def reduce_weight(dt, hx, hy, unit, beside):
    rows = dt.shape[0] // 8
    two = 2 * rows
    q, h = 2 * unit, 4 * unit
    one, pair, last = dt[:two], dt[two : 2 * two], dt[4 * two - rows :]
    m1 = mm(one, hx[:, h:]).astype(bf16)
    m2 = mm(pair, hx[:, q : q + h]).astype(bf16)
    t = mm(dt[2 * two : 4 * two - rows], hy).astype(bf16)
    m3, m4 = cat(t[:rows, h:], t[rows:two, :h], axis=1), t[two:]
    given, work, more = beside
    go, one, pair, last, *_ = stage(given, one, pair, last, m1, m2, m3, m4)
    ra, rb, rc, rd, a, b, d, *done = stage(
        xswap(m1, 1),
        xswap(m2, 3),
        yswap(m3, 1),
        yswap(m4, 3),
        mm(one, hx[:, q:h]),
        mm(pair, hx[:, q + h :]),
        mm(last, hy[:, h:]),
        *work(go),
    )
    m1 = (a + ra[:, :q]).astype(bf16)
    m2 = (b + rb[:, q:]).astype(bf16)
    m3 = t[rows:two, h:] + rc[:, h:]
    m4 = (d + rd[:, :h]).astype(bf16)
    go, one, pair, last, *_ = stage(go, one, pair, last, m1, m2, m3, m4)
    sa, sb, sc, sd, a, b, d, *later = stage(
        xswap(m1, 3),
        xswap(m2, 1),
        yswap(m3, 3),
        yswap(m4, 1),
        mm(one, hx[:, :q]),
        mm(pair, hx[:, :q]),
        mm(last, hy[:, :h]),
        *more(go),
    )
    ka = a + ra[:, q:] + sa
    kb = b + rb[:, :q] + sb
    kc = t[:rows, :h].astype(f32) + rc[:, :h] + sc
    kd = d + rd[:, h:] + sd
    ua = yswap(cat(ka[:rows, unit:], ka[rows:, :unit], axis=1).astype(bf16), 1)
    ub = yswap(kb[rows:].astype(bf16), 3)
    uc = xswap(kc[:, q:].astype(bf16), 1)
    ud = xswap(kd[:, unit : 3 * unit].astype(bf16), 3)
    va = yswap((ka[rows:, unit:] + ua[:, unit:]).astype(bf16), 3)
    vb = yswap((kb[:rows, unit:] + ub[:, :unit]).astype(bf16), 1)
    vc = xswap((kc[:, unit:q] + uc[:, :unit]).astype(bf16), 3)
    vd = xswap((kd[:, 3 * unit :] + ud[:, unit:]).astype(bf16), 1)
    out = [
        ka[:rows, :unit] + ua[:, :unit] + va,
        kb[:rows, :unit] + ub[:, unit:] + vb,
        kc[:, :unit] + uc[:, unit:] + vc,
        kd[:, :unit] + ud[:, :unit] + vd,
    ]
    first = stage(out[0], *done, *later)
    return [first[0]] + out[1:], first[1:]


def body(hidden_act, resid, w_down, norm_gain, w_proj, optical):
    tok_rows = hidden_act.shape[0]
    images = tok_rows // PATCHES
    width = resid.shape[1]
    half = width // 2
    shard = w_down.shape[0]
    cols = width // 32
    core, x, z, yl, yh = (lax.axis_index(a) for a in ("c", "x", "z", "yl", "yh"))

    opt_full = optical.astype(f32)
    opt_unit = (
        opt_full * lax.rsqrt(jnp.sum(opt_full * opt_full, axis=1, keepdims=True) + epsilon)
    ).astype(bf16)
    w_half = lax.dynamic_slice_in_dim(w_down, core * half, half, 1)
    near, near_peer, far, opt_own, both = gather(w_half, opt_unit, hidden_act, x, z, yl, yh)
    opt_peer = cswap(opt_own)

    def lanes(xr, yr):
        return lax.dynamic_slice_in_dim(both, ((yl ^ yr) * 4 + (x ^ xr)) * shard, shard, 1)

    pieces = {(xr, yr): lanes(xr, yr) for xr in range(4) for yr in range(2)}
    hx = cat(*[pieces[xr, yr] for xr in (0, 3, 2, 1) for yr in range(2)], axis=1)
    hy = cat(*[pieces[xr, yr] for yr in range(2) for xr in (0, 3, 2, 1)], axis=1)
    pick = turn(core, yh, z, width, cols)
    group = 4 * shard
    h_near = lax.dynamic_slice_in_dim(hidden_act, yl * group, group, 1)
    h_far = lax.dynamic_slice_in_dim(hidden_act, (1 - yl) * group, group, 1)
    branch_own, branch_peer = mm(h_near, near), mm(h_near, near_peer)
    far, hx, hy, pick, opt_own, branch_own, branch_peer, h_far = stage(
        far, hx, hy, pick, opt_own, branch_own, branch_peer, h_far
    )
    far_peer = cswap(far)
    branch_own = branch_own + mm(h_far, far)
    branch_peer = branch_peer + mm(h_far, far_peer)
    first = core == 0
    branch = cat(
        jnp.where(first, branch_own, branch_peer), jnp.where(first, branch_peer, branch_own), axis=1
    )
    summed = resid.astype(f32) + branch
    center = jnp.mean(summed, axis=1, keepdims=True)
    spread = jnp.mean((summed - center) ** 2, axis=1, keepdims=True)
    inv_std = lax.rsqrt(spread + epsilon)
    normed = (summed - center) * inv_std
    scaled = normed * norm_gain
    pooled = scaled.reshape(images, PATCHES, width).mean(axis=1).astype(bf16)
    embed = jnp.dot(pooled, w_proj, preferred_element_type=f32)
    inv_len = lax.rsqrt(jnp.sum(embed * embed, axis=1, keepdims=True) + epsilon)
    sar_unit = embed * inv_len
    sar_half = sar_unit.astype(bf16)
    scores = logit_scale * cat(
        *[
            lax.dot_general(sar_half, v, contract, preferred_element_type=f32)
            for v in (opt_own, opt_peer)
        ],
        axis=1,
    )
    pairs = scores.shape[1]
    powers = jnp.exp(scores)
    row_prob = powers / jnp.sum(powers, axis=1, keepdims=True)
    column = jnp.sum(powers, axis=0)
    totals = total_sum(column)
    col_prob = powers / totals
    first_pair = (((z * 2 + yh) * 2 + yl) * 4 + x) * images
    positive = (
        lax.broadcasted_iota(jnp.int32, scores.shape, 1)
        == first_pair + lax.broadcasted_iota(jnp.int32, scores.shape, 0)
    ).astype(f32)
    weights = (row_prob + col_prob - 2.0 * positive).astype(bf16)
    grad_unit = 0.5 * logit_scale * (
        mm(weights[:, : pairs // 2], opt_own) + mm(weights[:, pairs // 2 :], opt_peer)
    )
    grad_embed = inv_len * (
        grad_unit - sar_unit * jnp.sum(sar_unit * grad_unit, axis=1, keepdims=True)
    )
    grad_pooled = lax.dot_general(
        grad_embed.astype(bf16), w_proj, contract, preferred_element_type=f32
    )
    grad_tokens = jnp.broadcast_to(
        (grad_pooled / PATCHES)[:, None, :], (images, PATCHES, width)
    ).reshape(tok_rows, width)
    grad_normed = grad_tokens * norm_gain
    grad_sum = inv_std * (
        grad_normed
        - jnp.mean(grad_normed, axis=1, keepdims=True)
        - normed * jnp.mean(grad_normed * normed, axis=1, keepdims=True)
    )
    d_resid = grad_sum.astype(bf16)

    split, theirs = [
        lax.dot_general(v, d_resid, contract, preferred_element_type=f32).astype(bf16)
        for v in (pick[:half], pick[half:])
    ]
    dt = cat(split, cswap(theirs), axis=1)

    def hidden_grad(d, weights):
        d_own = lax.dynamic_slice_in_dim(d, core * half, half, 1)
        d_peer = lax.dynamic_slice_in_dim(d, (1 - core) * half, half, 1)
        return [
            (
                lax.dot_general(d_own, v, contract, preferred_element_type=f32)
                + lax.dot_general(d_peer, w, contract, preferred_element_type=f32)
            ).astype(bf16)
            for v, w in (weights,)
        ]

    parts, d_parts = reduce_weight(
        dt, hx, hy, shard, (
            d_resid,
            lambda d: hidden_grad(d, (near, near_peer)),
            lambda d: hidden_grad(d, (far, far_peer)),
        )
    )
    d_weight = parts[0][:cols]
    for flip in range(1, 8):
        block = parts[flip // 2][flip % 2 * cols :][:cols].astype(bf16)
        d_weight = d_weight + zswap(block, flip)
    a, b = d_parts
    d_hidden = cat(jnp.where(yl == 0, a, b), jnp.where(yl == 0, b, a), axis=1)
    return (d_hidden, d_resid, d_weight.T)


def solution(mesh):
    parts = Mesh(mesh.devices.reshape(2, -1, 2, 2, 4), ALL)
    rows = P(ALL, None)
    in_specs = (rows, rows, P(("yl", "x"), None), P(), P(), rows)
    out_specs = (rows, rows, P(("yl", "x"), ("yh", "z", "c")))
    return jax.shard_map(body, mesh=parts, in_specs=in_specs, out_specs=out_specs, check_vma=False)
```
